32 devices in a mesh: hid: 8 (over y, x, core), wid: 4 (over z).
Axes of the slice: x: 2, y: 2, z: 4, core: 2. Of those that a mesh axis runs over, the one named last changes fastest.
Arguments:
- tokens: bfloat16 [32, 16384], P('hid', 'wid'), may hold values from -6 to 6
- gate_weight: bfloat16 [16384, 26624], P('wid', 'hid'), may hold values from -0.046875 to 0.046875
- up_weight: bfloat16 [16384, 26624], P('wid', 'hid'), may hold values from -0.046875 to 0.046875
- down_weight: bfloat16 [26624, 16384], P('hid', 'wid'), may hold values from -0.0390625 to 0.0390625
Outputs:
- stream: bfloat16 [32, 16384], P('hid', 'wid')
The draws below stay inside these ranges and needn't reach their ends.
All inputs are finite; a program needn't handle non-finite values.
Results may differ from the reference program's by a relative error of at most 0.035.
Values may be sent and summed in bfloat16 or wider, within the bound.
A program may use at most 128 MiB of HBM per device.

```python
import jax
import jax.numpy as jnp
from jax import lax

D = 16384
FF = 26624
STEPS = 2
ROWS = 32
N_WID = 4


def shard_levels(own_key, shape, shards, low, high):
    factor_of, own = 1.0, jax.random.fold_in(own_key, 6)
    for dim, parts in shards:
        draws = jnp.exp(jax.random.uniform(jax.random.fold_in(own, dim), (parts,), jnp.float32, low / len(shards), high / len(shards)))
        factor_of = factor_of * jnp.repeat(draws, shape[dim] // parts).reshape([-1 if axis == dim else 1 for axis in range(len(shape))])
    return factor_of


def scatter_about(rng, dims, spread, bound, pieces=(), held_as=jnp.bfloat16):
    values = jax.random.normal(rng, dims, jnp.float32) * spread
    if len(pieces) > 0:
        values = shard_levels(rng, dims, pieces, -0.22, 0.18) * values
    return jnp.clip(values, min=-bound, max=bound).astype(held_as)


def setup_inputs(seed: int = 0) -> dict:
    arg_keys = jax.random.split(jax.random.key(seed), 5)
    tokens = scatter_about(arg_keys[0], (ROWS, D), 1.0, 6.0, ((0, 8), (1, 4)))
    gate_weight = scatter_about(arg_keys[1], (D, FF), D ** -0.5, 0.046875, ((0, 4), (1, 8)))
    up_weight = scatter_about(arg_keys[2], (D, FF), D ** -0.5, 0.046875, ((0, 4), (1, 8)))
    down_weight = scatter_about(arg_keys[3], (FF, D), FF ** -0.5, 0.0390625, ((0, 8), (1, 4)))
    return {"tokens": tokens, "gate_weight": gate_weight, "up_weight": up_weight, "down_weight": down_weight}


def reference(tokens, gate_weight, up_weight, down_weight):
    span_cols = D // N_WID
    stream = tokens
    for repeat in range(STEPS):
        def add_group(index, totals):
            offset = (index * span_cols).astype(jnp.int32)
            columns = lax.dynamic_slice_in_dim(stream, offset, span_cols, 1)
            gate_rows = lax.dynamic_slice_in_dim(gate_weight, offset, span_cols, 0)
            up_rows = lax.dynamic_slice_in_dim(up_weight, offset, span_cols, 0)
            gate_part = lax.optimization_barrier(jnp.dot(columns, gate_rows, preferred_element_type=jnp.float32).astype(jnp.bfloat16))
            up_part = lax.optimization_barrier(jnp.dot(columns, up_rows, preferred_element_type=jnp.float32).astype(jnp.bfloat16))
            return (totals[0] + gate_part.astype(jnp.float32), totals[1] + up_part.astype(jnp.float32))

        empty = jnp.zeros((stream.shape[0], gate_weight.shape[1]), jnp.float32)
        gate, up = lax.fori_loop(jnp.int32(0), jnp.int32(N_WID), add_group, (empty, empty))
        hidden = (jax.nn.silu(gate) * up).astype(jnp.bfloat16)
        branch = jnp.dot(hidden, down_weight, preferred_element_type=jnp.float32)
        stream = (stream.astype(jnp.float32) + branch).astype(jnp.bfloat16)
    return stream
```

```python
import functools

import jax
import jax.numpy as jnp
from jax import lax
from jax.experimental import pallas as pl
from jax.experimental.pallas import tpu as pltpu
from jax.sharding import PartitionSpec as P

STEPS = 2
MESH = pl.DeviceIdType.MESH
LANES = 128
TALL = 16
UNITS = 256
KEEP = 5
RING = 9
LAG = 4


def activate(partial_value):
    totals = lax.psum(partial_value.astype(jnp.bfloat16), "wid").astype(jnp.float32)
    return (jax.nn.silu(totals[:, 0]) * totals[:, 1]).astype(jnp.bfloat16)


def plain(tokens, gate_weight, up_weight, down_weight):
    stream = tokens
    for repeat in range(STEPS):
        shard_rows = lax.all_gather(stream, "hid", axis=0, tiled=True)
        gate_part = jnp.dot(shard_rows, gate_weight, preferred_element_type=jnp.float32)
        up_part = jnp.dot(shard_rows, up_weight, preferred_element_type=jnp.float32)
        partial_value = jnp.stack([gate_part, up_part], axis=1)
        hidden = activate(partial_value)
        branch = lax.psum_scatter(
            jnp.dot(hidden, down_weight, preferred_element_type=jnp.float32),
            "hid",
            scatter_dimension=0,
            tiled=True,
        )
        stream = (stream.astype(jnp.float32) + branch).astype(jnp.bfloat16)
    return stream


def landed(ref, sem):
    pltpu.make_async_copy(ref, ref, sem).wait()


def kernel(
    n_hid, n_wid, keep, ring, lag,
    tok_ref, gate_ref, up_ref, down_ref, out_ref,
    slots, x_wide, x_all, x_got, own, product, p_send, p_got, h_got, h_all,
    branch, d_send, d_got, d_own, out_wide,
    slot_sem, x_sems, p_send_sem, p_sem, h_sems, d_sems,
):
    f32, bf16 = jnp.float32, jnp.bfloat16
    hid, wid = lax.axis_index("hid"), lax.axis_index("wid")
    rows, width = tok_ref.shape
    hidden = gate_ref.shape[1]
    fold = TALL // rows
    cols = fold * LANES
    n_up, n_down = hidden // UNITS, width // cols
    group = TALL // 2
    streamed = n_up - keep + n_down

    def fetch_up(j, slot):
        off = pl.ds(pl.multiple_of(j * UNITS, UNITS), UNITS)
        return [
            pltpu.make_async_copy(
                ref.at[:, off],
                slots.at[slot, pl.ds(0, width), pl.ds(half * UNITS, UNITS)],
                slot_sem.at[slot, half],
            )
            for half, ref in enumerate((gate_ref, up_ref))
        ]

    def fetch_down(c, slot):
        off = pl.ds(pl.multiple_of(c * cols, cols), cols)
        return pltpu.make_async_copy(
            down_ref.at[:, off], slots.at[slot, pl.ds(0, hidden), :], slot_sem.at[slot, 0]
        )

    def start(q):
        slot = keep + q % ring
        k = q % streamed + keep

        @pl.when(jnp.logical_and(q < STEPS * streamed, k < n_up))
        def _():
            for copy in fetch_up(k, slot):
                copy.start()

        @pl.when(jnp.logical_and(q < STEPS * streamed, k >= n_up))
        def _():
            fetch_down(k - n_up, slot).start()

    @pl.loop(0, keep)
    def _(j):
        for copy in fetch_up(j, j):
            copy.start()

    @pl.loop(0, ring)
    def _(q):
        start(q)

    barrier = pltpu.get_barrier_semaphore()

    for d in range(1, n_hid):
        pl.semaphore_signal(
            barrier, inc=1, device_id=((hid + d) % n_hid, wid), device_id_type=MESH
        )
    for d in range(1, n_wid):
        pl.semaphore_signal(
            barrier, inc=1, device_id=(hid, (wid + d) % n_wid), device_id_type=MESH
        )

    for c in range(n_down):
        for f in range(fold):
            off = c * cols + f * LANES
            own[c, f * rows:(f + 1) * rows, :] = tok_ref[:, off:off + LANES].astype(f32)

    pl.semaphore_wait(barrier, n_hid + n_wid - 2)

    def step(s, carry):
        x_got[s, hid] = own[...].astype(bf16)
        for d in range(1, n_hid):
            pltpu.make_async_remote_copy(
                src_ref=x_got.at[s, hid],
                dst_ref=x_got.at[s, hid],
                send_sem=x_sems.at[s, 0],
                recv_sem=x_sems.at[s, 1],
                device_id=((hid + d) % n_hid, wid),
                device_id_type=MESH,
            ).start()
        landed(x_got.at[s, pl.ds(0, n_hid - 1)], x_sems.at[s, 1])
        for h in range(n_hid):
            for c in range(n_down):
                block = x_got[s, h, c].astype(f32)
                for f in range(fold):
                    off = c * cols + f * LANES
                    x_wide[h * rows:(h + 1) * rows, off:off + LANES] = block[
                        f * rows:(f + 1) * rows, :
                    ]
        x_all[...] = x_wide[...].astype(bf16)

        def finish(j):
            landed(p_got.at[s, j], p_sem.at[s, j])
            total = p_send[s, j, wid].astype(f32)
            for d in range(n_wid - 1):
                total = total + p_got[s, j, d].astype(f32)
            gate, up = total[:group, :], total[group:, :]
            value = gate / (1.0 + jnp.exp(-gate)) * up
            h_got[s, j, wid] = jnp.concatenate(
                [value[:, :LANES], value[:, LANES:]], axis=0
            ).astype(bf16)
            for d in range(1, n_wid):
                pltpu.make_async_remote_copy(
                    src_ref=h_got.at[s, j, wid],
                    dst_ref=h_got.at[s, j, wid],
                    send_sem=h_sems.at[s, 0],
                    recv_sem=h_sems.at[s, 1],
                    device_id=(hid, (wid + d) % n_wid),
                    device_id_type=MESH,
                ).start()

        @pl.loop(0, n_up)
        def _(j):
            q = s * streamed + j - keep
            kept = j < keep
            slot = jnp.where(kept, j, keep + (q + ring) % ring)

            @pl.when(jnp.logical_or(s == 0, jnp.logical_not(kept)))
            def _():
                for copy in fetch_up(j, slot):
                    copy.wait()

            product[...] = jnp.dot(
                x_all[...], slots[slot, :width, :], preferred_element_type=f32
            )
            for w in range(n_wid):
                lo = w * group
                p_send[s, j, w] = jnp.concatenate(
                    [product[lo:lo + group, :UNITS], product[lo:lo + group, UNITS:]], axis=0
                ).astype(bf16)
            for d in range(1, n_wid):
                peer = (wid + d) % n_wid
                pltpu.make_async_remote_copy(
                    src_ref=p_send.at[s, j, peer],
                    dst_ref=p_got.at[s, j, d - 1],
                    send_sem=p_send_sem.at[s],
                    recv_sem=p_sem.at[s, j],
                    device_id=(hid, peer),
                    device_id_type=MESH,
                ).start()

            @pl.when(jnp.logical_not(kept))
            def _():
                start(q + ring)

            @pl.when(j >= lag)
            def _():
                finish(j - lag)

        @pl.loop(n_up - lag, n_up)
        def _(j):
            finish(j)

        landed(h_got.at[s, :, pl.ds(0, n_wid - 1)], h_sems.at[s, 1])
        for j in range(n_up):
            block = h_got[s, j].astype(f32)
            for half in range(2):
                off = j * UNITS + half * LANES
                h_all[:, off:off + LANES] = (
                    block[:, half * group:(half + 1) * group, :]
                    .reshape(n_wid * group, LANES)
                    .astype(bf16)
                )

        @pl.loop(0, n_down)
        def _(c):
            q = s * streamed + n_up - keep + c
            slot = keep + q % ring
            fetch_down(c, slot).wait()
            x_wide[:, :cols] = jnp.dot(
                h_all[...], slots[slot, :hidden, :], preferred_element_type=f32
            )
            for h in range(n_hid):
                for f in range(fold):
                    branch[h, f * rows:(f + 1) * rows, :] = x_wide[
                        h * rows:(h + 1) * rows, f * LANES:(f + 1) * LANES
                    ]
            d_send[s, c] = branch[...].astype(bf16)
            d_own[c] = branch[hid]
            for d in range(1, n_hid):
                peer = (hid + d) % n_hid
                pltpu.make_async_remote_copy(
                    src_ref=d_send.at[s, c, peer],
                    dst_ref=d_got.at[s, c, d - 1],
                    send_sem=d_sems.at[s, 0],
                    recv_sem=d_sems.at[s, 1],
                    device_id=(peer, wid),
                    device_id_type=MESH,
                ).start()
            start(q + ring)

        landed(d_got.at[s], d_sems.at[s, 1])
        total = d_own[...]
        for d in range(n_hid - 1):
            total = total + d_got[s, :, d].astype(f32)
        own[...] = (own[...] + total).astype(bf16).astype(f32)

        landed(x_got.at[s, pl.ds(0, n_hid - 1)], x_sems.at[s, 0])
        landed(p_send.at[s, :, pl.ds(0, n_wid - 1)], p_send_sem.at[s])
        landed(h_got.at[s, :, pl.ds(0, n_wid - 1)], h_sems.at[s, 0])
        landed(d_send.at[s, :, pl.ds(0, n_hid - 1)], d_sems.at[s, 0])
        return carry

    lax.fori_loop(0, STEPS, step, 0)

    for c in range(n_down):
        for f in range(fold):
            off = c * cols + f * LANES
            out_wide[:, off:off + LANES] = own[c, f * rows:(f + 1) * rows, :]
    out_ref[...] = out_wide[...].astype(bf16)


def fused(n_hid, n_wid, tokens, gate_weight, up_weight, down_weight):
    rows, width = tokens.shape
    hidden = gate_weight.shape[1]
    fold = TALL // rows
    cols = fold * LANES
    n_up, n_down = hidden // UNITS, width // cols
    keep = min(KEEP, n_up - 1)
    ring = min(RING, n_up - keep + n_down)
    lag = min(LAG, n_up - 1)
    all_rows = n_hid * rows
    bf16, f32 = jnp.bfloat16, jnp.float32
    dma = pltpu.SemaphoreType.DMA
    weights = 3 * width * hidden
    return pl.pallas_call(
        functools.partial(kernel, n_hid, n_wid, keep, ring, lag),
        out_shape=jax.ShapeDtypeStruct((rows, width), bf16),
        in_specs=[pl.BlockSpec(memory_space=pltpu.VMEM)]
        + [pl.BlockSpec(memory_space=pl.ANY)] * 3,
        out_specs=pl.BlockSpec(memory_space=pltpu.VMEM),
        scratch_shapes=[
            pltpu.VMEM((keep + ring, max(width, hidden), 2 * UNITS), bf16),
            pltpu.VMEM((all_rows, width), f32),
            pltpu.VMEM((all_rows, width), bf16),
            pltpu.VMEM((STEPS, n_hid, n_down, TALL, LANES), bf16),
            pltpu.VMEM((n_down, TALL, LANES), f32),
            pltpu.VMEM((all_rows, 2 * UNITS), f32),
            pltpu.VMEM((STEPS, n_up, n_wid, TALL, UNITS), bf16),
            pltpu.VMEM((STEPS, n_up, n_wid - 1, TALL, UNITS), bf16),
            pltpu.VMEM((STEPS, n_up, n_wid, TALL, LANES), bf16),
            pltpu.VMEM((all_rows, hidden), bf16),
            pltpu.VMEM((n_hid, TALL, LANES), f32),
            pltpu.VMEM((STEPS, n_down, n_hid, TALL, LANES), bf16),
            pltpu.VMEM((STEPS, n_down, n_hid - 1, TALL, LANES), bf16),
            pltpu.VMEM((n_down, TALL, LANES), f32),
            pltpu.VMEM((rows, width), f32),
            dma((keep + ring, 2)),
            dma((STEPS, 2)),
            dma((STEPS,)),
            dma((STEPS, n_up)),
            dma((STEPS, 2)),
            dma((STEPS, 2)),
        ],
        compiler_params=pltpu.CompilerParams(
            collective_id=0, has_side_effects=True, vmem_limit_bytes=VMEM_BYTES
        ),
        cost_estimate=pl.CostEstimate(
            flops=STEPS * 2 * all_rows * weights,
            bytes_accessed=STEPS * 2 * weights,
            transcendentals=STEPS * all_rows * hidden,
        ),
    )(tokens, gate_weight, up_weight, down_weight)


VMEM_BYTES = 64 * 1024 * 1024 - 64 * 1024


def per_device(n_hid, n_wid, tokens, gate_weight, up_weight, down_weight):
    rows, width = tokens.shape
    hidden = gate_weight.shape[1]
    fits = (
        TALL % rows == 0
        and n_hid > 1
        and n_wid > 1
        and n_hid * rows == n_wid * (TALL // 2)
        and hidden % UNITS == 0
        and hidden >= 2 * UNITS
        and (TALL // rows) * LANES == 2 * UNITS
        and width % (2 * UNITS) == 0
    )
    if fits:
        return fused(n_hid, n_wid, tokens, gate_weight, up_weight, down_weight)
    return plain(tokens, gate_weight, up_weight, down_weight)


def solution(mesh):
    in_specs = (P("hid", "wid"), P("wid", "hid"), P("wid", "hid"), P("hid", "wid"))
    out_specs = P("hid", "wid")
    return jax.shard_map(
        functools.partial(per_device, mesh.shape["hid"], mesh.shape["wid"]),
        mesh=mesh,
        in_specs=in_specs,
        out_specs=out_specs,
        check_vma=False,
    )
```

```python
import functools

import jax
import jax.numpy as jnp
from jax import lax
from jax.experimental import pallas as pl
from jax.experimental.pallas import tpu as pltpu
from jax.sharding import PartitionSpec as P

STEPS = 2
MESH = pl.DeviceIdType.MESH
LANES = 128
TALL = 16
UNITS = 256
KEEP = 5
RING = 9
LAG = 3


def activate(partial_value):
    totals = lax.psum(partial_value.astype(jnp.bfloat16), "wid").astype(jnp.float32)
    return (jax.nn.silu(totals[:, 0]) * totals[:, 1]).astype(jnp.bfloat16)


def plain(tokens, gate_weight, up_weight, down_weight):
    stream = tokens
    for repeat in range(STEPS):
        shard_rows = lax.all_gather(stream, "hid", axis=0, tiled=True)
        gate_part = jnp.dot(shard_rows, gate_weight, preferred_element_type=jnp.float32)
        up_part = jnp.dot(shard_rows, up_weight, preferred_element_type=jnp.float32)
        partial_value = jnp.stack([gate_part, up_part], axis=1)
        hidden = activate(partial_value)
        branch = lax.psum_scatter(
            jnp.dot(hidden, down_weight, preferred_element_type=jnp.float32),
            "hid",
            scatter_dimension=0,
            tiled=True,
        )
        stream = (stream.astype(jnp.float32) + branch).astype(jnp.bfloat16)
    return stream


def landed(ref, sem):
    pltpu.make_async_copy(ref, ref, sem).wait()


def kernel(
    n_hid, n_wid, keep, ring, lag, early,
    tok_ref, gate_ref, up_ref, down_ref, out_ref,
    slots, x_wide, x_all, x_got, own, product, p_send, p_got, h_got, h_all,
    partial, branch, d_send, d_got, d_own, out_wide,
    slot_sem, x_sems, p_send_sem, p_sem, h_sems, d_sems,
):
    f32, bf16 = jnp.float32, jnp.bfloat16
    hid, wid = lax.axis_index("hid"), lax.axis_index("wid")
    rows, width = tok_ref.shape
    hidden = gate_ref.shape[1]
    fold = TALL // rows
    cols = fold * LANES
    n_up, n_down = hidden // UNITS, width // cols
    group = TALL // 2
    n_pair = n_down // 2
    streamed = n_up - keep + 2 * n_pair
    k_early, k_late = early * UNITS, hidden - early * UNITS

    def fetch_up(j, slot):
        off = pl.ds(pl.multiple_of(j * UNITS, UNITS), UNITS)
        return [
            pltpu.make_async_copy(
                ref.at[:, off],
                slots.at[slot, pl.ds(0, width), pl.ds(half * UNITS, UNITS)],
                slot_sem.at[slot, half],
            )
            for half, ref in enumerate((gate_ref, up_ref))
        ]

    def fetch_down(c, slot, late):
        top, depth = (k_early, k_late) if late else (0, k_early)
        return [
            pltpu.make_async_copy(
                down_ref.at[
                    pl.ds(top, depth),
                    pl.ds(pl.multiple_of((2 * c + half) * cols, cols), cols),
                ],
                slots.at[slot, pl.ds(half * depth, depth), :],
                slot_sem.at[slot, half],
            )
            for half in range(2)
        ]

    def start(q):
        slot = keep + q % ring
        k = q % streamed + keep

        @pl.when(jnp.logical_and(q < STEPS * streamed, k < n_up))
        def _():
            for copy in fetch_up(k, slot):
                copy.start()

        in_early = jnp.logical_and(k >= n_up, k < n_up + n_pair)

        @pl.when(jnp.logical_and(q < STEPS * streamed, in_early))
        def _():
            for copy in fetch_down(k - n_up, slot, False):
                copy.start()

        @pl.when(jnp.logical_and(q < STEPS * streamed, k >= n_up + n_pair))
        def _():
            for copy in fetch_down(k - n_up - n_pair, slot, True):
                copy.start()

    @pl.loop(0, keep)
    def _(j):
        for copy in fetch_up(j, j):
            copy.start()

    @pl.loop(0, ring)
    def _(q):
        start(q)

    barrier = pltpu.get_barrier_semaphore()

    for d in range(1, n_hid):
        pl.semaphore_signal(
            barrier, inc=1, device_id=((hid + d) % n_hid, wid), device_id_type=MESH
        )
    for d in range(1, n_wid):
        pl.semaphore_signal(
            barrier, inc=1, device_id=(hid, (wid + d) % n_wid), device_id_type=MESH
        )

    for c in range(n_down):
        for f in range(fold):
            off = c * cols + f * LANES
            own[c, f * rows:(f + 1) * rows, :] = tok_ref[:, off:off + LANES].astype(f32)

    pl.semaphore_wait(barrier, n_hid + n_wid - 2)

    def step(s, carry):
        x_got[s, hid] = own[...].astype(bf16)
        for d in range(1, n_hid):
            pltpu.make_async_remote_copy(
                src_ref=x_got.at[s, hid],
                dst_ref=x_got.at[s, hid],
                send_sem=x_sems.at[s, 0],
                recv_sem=x_sems.at[s, 1],
                device_id=((hid + d) % n_hid, wid),
                device_id_type=MESH,
            ).start()
        landed(x_got.at[s, pl.ds(0, n_hid - 1)], x_sems.at[s, 1])
        for h in range(n_hid):
            for c in range(n_down):
                block = x_got[s, h, c].astype(f32)
                for f in range(fold):
                    off = c * cols + f * LANES
                    x_wide[h * rows:(h + 1) * rows, off:off + LANES] = block[
                        f * rows:(f + 1) * rows, :
                    ]
        x_all[...] = x_wide[...].astype(bf16)

        def finish(j):
            total = p_send[s, j, wid].astype(f32)
            for d in range(n_wid - 1):
                total = total + p_got[s, j, d].astype(f32)
            gate, up = total[:group, :], total[group:, :]
            value = gate / (1.0 + jnp.exp(-gate)) * up
            h_got[s, j, wid] = jnp.concatenate(
                [value[:, :LANES], value[:, LANES:]], axis=0
            ).astype(bf16)

        def share(j):
            late = jnp.where(j >= early, 1, 0)
            for d in range(1, n_wid):
                pltpu.make_async_remote_copy(
                    src_ref=h_got.at[s, j, wid],
                    dst_ref=h_got.at[s, j, wid],
                    send_sem=h_sems.at[s, 2],
                    recv_sem=h_sems.at[s, late],
                    device_id=(hid, (wid + d) % n_wid),
                    device_id_type=MESH,
                ).start()

        def piece(j, with_finish):
            q = s * streamed + j - keep
            kept = j < keep
            slot = jnp.where(kept, j, keep + (q + ring) % ring)

            @pl.when(jnp.logical_or(s == 0, jnp.logical_not(kept)))
            def _():
                for copy in fetch_up(j, slot):
                    copy.wait()

            if with_finish:
                landed(p_got.at[s, j - lag], p_sem.at[s, j - lag])
                finish(j - lag)
            product[...] = jnp.dot(
                x_all[...], slots[slot, :width, :], preferred_element_type=f32
            )
            for w in range(n_wid):
                lo = w * group
                p_send[s, j, w] = jnp.concatenate(
                    [product[lo:lo + group, :UNITS], product[lo:lo + group, UNITS:]], axis=0
                ).astype(bf16)
            for d in range(1, n_wid):
                peer = (wid + d) % n_wid
                pltpu.make_async_remote_copy(
                    src_ref=p_send.at[s, j, peer],
                    dst_ref=p_got.at[s, j, d - 1],
                    send_sem=p_send_sem.at[s],
                    recv_sem=p_sem.at[s, j],
                    device_id=(hid, peer),
                    device_id_type=MESH,
                ).start()
            if with_finish:
                share(j - lag)

            @pl.when(jnp.logical_not(kept))
            def _():
                start(q + ring)

        @pl.loop(0, lag)
        def _(j):
            piece(j, False)

        @pl.loop(lag, n_up)
        def _(j):
            piece(j, True)

        def gather_hidden(first, last, sem):
            landed(
                h_got.at[s, pl.ds(first, last - first), pl.ds(0, n_wid - 1)],
                h_sems.at[s, sem],
            )
            for j in range(first, last):
                block = h_got[s, j].astype(f32)
                for half in range(2):
                    off = j * UNITS + half * LANES
                    h_all[:, off:off + LANES] = (
                        block[:, half * group:(half + 1) * group, :]
                        .reshape(n_wid * group, LANES)
                        .astype(bf16)
                    )

        gather_hidden(0, early, 0)

        def early_pair(c, with_finish):
            q = s * streamed + n_up - keep + c
            slot = keep + q % ring
            for copy in fetch_down(c, slot, False):
                copy.wait()
            if with_finish:
                j = n_up - lag + c
                landed(p_got.at[s, j], p_sem.at[s, j])
                finish(j)
            for half in range(2):
                lo = half * k_early
                partial[2 * c + half] = jnp.dot(
                    h_all[:, :k_early],
                    slots[slot, lo:lo + k_early, :],
                    preferred_element_type=f32,
                )
            if with_finish:
                share(j)
            start(q + ring)

        both = min(lag, n_pair)

        @pl.loop(0, both)
        def _(c):
            early_pair(c, True)

        @pl.loop(both, n_pair)
        def _(c):
            early_pair(c, False)

        @pl.loop(n_up - lag + both, n_up)
        def _(j):
            landed(p_got.at[s, j], p_sem.at[s, j])
            finish(j)
            share(j)

        gather_hidden(early, n_up, 1)

        @pl.loop(0, n_pair)
        def _(pair):
            q = s * streamed + n_up - keep + n_pair + pair
            slot = keep + q % ring
            for copy in fetch_down(pair, slot, True):
                copy.wait()
            for half in range(2):
                c = 2 * pair + half
                lo = half * k_late
                x_wide[:, :cols] = partial[c] + jnp.dot(
                    h_all[:, k_early:],
                    slots[slot, lo:lo + k_late, :],
                    preferred_element_type=f32,
                )
                for h in range(n_hid):
                    for f in range(fold):
                        branch[h, f * rows:(f + 1) * rows, :] = x_wide[
                            h * rows:(h + 1) * rows, f * LANES:(f + 1) * LANES
                        ]
                d_send[s, c] = branch[...].astype(bf16)
                d_own[c] = branch[hid]
                for d in range(1, n_hid):
                    peer = (hid + d) % n_hid
                    pltpu.make_async_remote_copy(
                        src_ref=d_send.at[s, c, peer],
                        dst_ref=d_got.at[s, c, d - 1],
                        send_sem=d_sems.at[s, 0],
                        recv_sem=d_sems.at[s, 1],
                        device_id=(peer, wid),
                        device_id_type=MESH,
                    ).start()
            start(q + ring)

        landed(d_got.at[s], d_sems.at[s, 1])
        total = d_own[...]
        for d in range(n_hid - 1):
            total = total + d_got[s, :, d].astype(f32)
        own[...] = (own[...] + total).astype(bf16).astype(f32)

        landed(x_got.at[s, pl.ds(0, n_hid - 1)], x_sems.at[s, 0])
        landed(p_send.at[s, :, pl.ds(0, n_wid - 1)], p_send_sem.at[s])
        landed(h_got.at[s, :, pl.ds(0, n_wid - 1)], h_sems.at[s, 2])
        landed(d_send.at[s, :, pl.ds(0, n_hid - 1)], d_sems.at[s, 0])
        return carry

    lax.fori_loop(0, STEPS, step, 0)

    for c in range(n_down):
        for f in range(fold):
            off = c * cols + f * LANES
            out_wide[:, off:off + LANES] = own[c, f * rows:(f + 1) * rows, :]
    out_ref[...] = out_wide[...].astype(bf16)


def fused(n_hid, n_wid, tokens, gate_weight, up_weight, down_weight):
    rows, width = tokens.shape
    hidden = gate_weight.shape[1]
    fold = TALL // rows
    cols = fold * LANES
    n_up, n_down = hidden // UNITS, width // cols
    keep = min(KEEP, n_up - 1)
    ring = min(RING, n_up - keep + n_down)
    lag = min(LAG, n_up - 1)
    early = max(1, n_up * 5 // 8)
    slot_rows = max(width, 2 * UNITS * max(early, n_up - early))
    all_rows = n_hid * rows
    bf16, f32 = jnp.bfloat16, jnp.float32
    dma = pltpu.SemaphoreType.DMA
    weights = 3 * width * hidden
    return pl.pallas_call(
        functools.partial(kernel, n_hid, n_wid, keep, ring, lag, early),
        out_shape=jax.ShapeDtypeStruct((rows, width), bf16),
        in_specs=[pl.BlockSpec(memory_space=pltpu.VMEM)]
        + [pl.BlockSpec(memory_space=pl.ANY)] * 3,
        out_specs=pl.BlockSpec(memory_space=pltpu.VMEM),
        scratch_shapes=[
            pltpu.VMEM((keep + ring, slot_rows, 2 * UNITS), bf16),
            pltpu.VMEM((all_rows, width), f32),
            pltpu.VMEM((all_rows, width), bf16),
            pltpu.VMEM((STEPS, n_hid, n_down, TALL, LANES), bf16),
            pltpu.VMEM((n_down, TALL, LANES), f32),
            pltpu.VMEM((all_rows, 2 * UNITS), f32),
            pltpu.VMEM((STEPS, n_up, n_wid, TALL, UNITS), bf16),
            pltpu.VMEM((STEPS, n_up, n_wid - 1, TALL, UNITS), bf16),
            pltpu.VMEM((STEPS, n_up, n_wid, TALL, LANES), bf16),
            pltpu.VMEM((all_rows, hidden), bf16),
            pltpu.VMEM((n_down, all_rows, cols), f32),
            pltpu.VMEM((n_hid, TALL, LANES), f32),
            pltpu.VMEM((STEPS, n_down, n_hid, TALL, LANES), bf16),
            pltpu.VMEM((STEPS, n_down, n_hid - 1, TALL, LANES), bf16),
            pltpu.VMEM((n_down, TALL, LANES), f32),
            pltpu.VMEM((rows, width), f32),
            dma((keep + ring, 2)),
            dma((STEPS, 2)),
            dma((STEPS,)),
            dma((STEPS, n_up)),
            dma((STEPS, 3)),
            dma((STEPS, 2)),
        ],
        compiler_params=pltpu.CompilerParams(
            collective_id=0, has_side_effects=True, vmem_limit_bytes=VMEM_BYTES
        ),
        cost_estimate=pl.CostEstimate(
            flops=STEPS * 2 * all_rows * weights,
            bytes_accessed=STEPS * 2 * weights,
            transcendentals=STEPS * all_rows * hidden,
        ),
    )(tokens, gate_weight, up_weight, down_weight)


VMEM_BYTES = 64 * 1024 * 1024 - 64 * 1024


def per_device(n_hid, n_wid, tokens, gate_weight, up_weight, down_weight):
    rows, width = tokens.shape
    hidden = gate_weight.shape[1]
    fits = (
        TALL % rows == 0
        and n_hid > 1
        and n_wid > 1
        and n_hid * rows == n_wid * (TALL // 2)
        and hidden % UNITS == 0
        and hidden >= 2 * UNITS
        and (TALL // rows) * LANES == 2 * UNITS
        and width % (4 * UNITS) == 0
    )
    if fits:
        return fused(n_hid, n_wid, tokens, gate_weight, up_weight, down_weight)
    return plain(tokens, gate_weight, up_weight, down_weight)


def solution(mesh):
    in_specs = (P("hid", "wid"), P("wid", "hid"), P("wid", "hid"), P("hid", "wid"))
    out_specs = P("hid", "wid")
    return jax.shard_map(
        functools.partial(per_device, mesh.shape["hid"], mesh.shape["wid"]),
        mesh=mesh,
        in_specs=in_specs,
        out_specs=out_specs,
        check_vma=False,
    )
```

```python
import functools

import jax
import jax.numpy as jnp
from jax import lax
from jax.experimental import pallas as pl
from jax.experimental.pallas import tpu as pltpu
from jax.sharding import PartitionSpec as P

STEPS = 2
MESH = pl.DeviceIdType.MESH
LANES = 128
TALL = 16
UNITS = 256
KEEP = 5
RING = 9
LAG = 5


def activate(partial_value):
    totals = lax.psum(partial_value.astype(jnp.bfloat16), "wid").astype(jnp.float32)
    return (jax.nn.silu(totals[:, 0]) * totals[:, 1]).astype(jnp.bfloat16)


def plain(tokens, gate_weight, up_weight, down_weight):
    stream = tokens
    for repeat in range(STEPS):
        shard_rows = lax.all_gather(stream, "hid", axis=0, tiled=True)
        gate_part = jnp.dot(shard_rows, gate_weight, preferred_element_type=jnp.float32)
        up_part = jnp.dot(shard_rows, up_weight, preferred_element_type=jnp.float32)
        partial_value = jnp.stack([gate_part, up_part], axis=1)
        hidden = activate(partial_value)
        branch = lax.psum_scatter(
            jnp.dot(hidden, down_weight, preferred_element_type=jnp.float32),
            "hid",
            scatter_dimension=0,
            tiled=True,
        )
        stream = (stream.astype(jnp.float32) + branch).astype(jnp.bfloat16)
    return stream


def landed(ref, sem):
    pltpu.make_async_copy(ref, ref, sem).wait()


def kernel(
    n_hid, n_wid, keep, ring, lag, levels,
    tok_ref, gate_ref, up_ref, down_ref, out_ref,
    slots, x_wide, x_all, x_got, own, product, p_send, p_got, h_got, h_all,
    partial, branch, d_send, d_got, d_own, out_wide,
    slot_sem, x_sems, p_send_sem, p_sem, h_sems, d_sems,
):
    f32, bf16 = jnp.float32, jnp.bfloat16
    hid, wid = lax.axis_index("hid"), lax.axis_index("wid")
    rows, width = tok_ref.shape
    hidden = gate_ref.shape[1]
    fold = TALL // rows
    cols = fold * LANES
    n_up, n_down = hidden // UNITS, width // cols
    group = TALL // 2
    streamed = n_up - keep + levels[-1][3] + levels[-1][4]

    def fetch_up(j, slot):
        off = pl.ds(pl.multiple_of(j * UNITS, UNITS), UNITS)
        return [
            pltpu.make_async_copy(
                ref.at[:, off],
                slots.at[slot, pl.ds(0, width), pl.ds(half * UNITS, UNITS)],
                slot_sem.at[slot, half],
            )
            for half, ref in enumerate((gate_ref, up_ref))
        ]

    def fetch_down(u, slot, level):
        first, last, per = level[:3]
        depth = (last - first) * UNITS
        return [
            pltpu.make_async_copy(
                down_ref.at[
                    pl.ds(first * UNITS, depth),
                    pl.ds(pl.multiple_of((per * u + part) * cols, cols), cols),
                ],
                slots.at[slot, pl.ds(part * depth, depth), :],
                slot_sem.at[slot, part],
            )
            for part in range(per)
        ]

    def start(q):
        slot = keep + q % ring
        k = q % streamed + keep

        @pl.when(jnp.logical_and(q < STEPS * streamed, k < n_up))
        def _():
            for copy in fetch_up(k, slot):
                copy.start()

        for level in levels:
            u = k - n_up - level[4]
            here = jnp.logical_and(u >= 0, u < level[3])

            @pl.when(jnp.logical_and(q < STEPS * streamed, here))
            def _():
                for copy in fetch_down(u, slot, level):
                    copy.start()

    @pl.loop(0, keep)
    def _(j):
        for copy in fetch_up(j, j):
            copy.start()

    @pl.loop(0, ring)
    def _(q):
        start(q)

    barrier = pltpu.get_barrier_semaphore()

    for d in range(1, n_hid):
        pl.semaphore_signal(
            barrier, inc=1, device_id=((hid + d) % n_hid, wid), device_id_type=MESH
        )
    for d in range(1, n_wid):
        pl.semaphore_signal(
            barrier, inc=1, device_id=(hid, (wid + d) % n_wid), device_id_type=MESH
        )

    for c in range(n_down):
        for f in range(fold):
            off = c * cols + f * LANES
            own[c, f * rows:(f + 1) * rows, :] = tok_ref[:, off:off + LANES].astype(f32)

    pl.semaphore_wait(barrier, n_hid + n_wid - 2)

    def step(s, carry):
        x_got[s, hid] = own[...].astype(bf16)
        for d in range(1, n_hid):
            pltpu.make_async_remote_copy(
                src_ref=x_got.at[s, hid],
                dst_ref=x_got.at[s, hid],
                send_sem=x_sems.at[s, 0],
                recv_sem=x_sems.at[s, 1],
                device_id=((hid + d) % n_hid, wid),
                device_id_type=MESH,
            ).start()
        landed(x_got.at[s, pl.ds(0, n_hid - 1)], x_sems.at[s, 1])
        for h in range(n_hid):
            for c in range(n_down):
                block = x_got[s, h, c].astype(f32)
                for f in range(fold):
                    off = c * cols + f * LANES
                    x_wide[h * rows:(h + 1) * rows, off:off + LANES] = block[
                        f * rows:(f + 1) * rows, :
                    ]
        x_all[...] = x_wide[...].astype(bf16)

        def finish(j):
            total = p_send[s, j, wid].astype(f32)
            for d in range(n_wid - 1):
                total = total + p_got[s, j, d].astype(f32)
            gate, up = total[:group, :], total[group:, :]
            value = gate / (1.0 + jnp.exp(-gate)) * up
            h_got[s, j, wid] = jnp.concatenate(
                [value[:, :LANES], value[:, LANES:]], axis=0
            ).astype(bf16)

        def share(j):
            level_of = sum(jnp.where(j >= level[0], 1, 0) for level in levels[1:])
            for d in range(1, n_wid):
                pltpu.make_async_remote_copy(
                    src_ref=h_got.at[s, j, wid],
                    dst_ref=h_got.at[s, j, wid],
                    send_sem=h_sems.at[s, len(levels)],
                    recv_sem=h_sems.at[s, level_of],
                    device_id=(hid, (wid + d) % n_wid),
                    device_id_type=MESH,
                ).start()

        def piece(j, with_finish):
            q = s * streamed + j - keep
            kept = j < keep
            slot = jnp.where(kept, j, keep + (q + ring) % ring)

            @pl.when(jnp.logical_or(s == 0, jnp.logical_not(kept)))
            def _():
                for copy in fetch_up(j, slot):
                    copy.wait()

            if with_finish:
                landed(p_got.at[s, j - lag], p_sem.at[s, j - lag])
                finish(j - lag)
            product[...] = jnp.dot(
                x_all[...], slots[slot, :width, :], preferred_element_type=f32
            )
            for w in range(n_wid):
                lo = w * group
                p_send[s, j, w] = jnp.concatenate(
                    [product[lo:lo + group, :UNITS], product[lo:lo + group, UNITS:]], axis=0
                ).astype(bf16)
            for d in range(1, n_wid):
                peer = (wid + d) % n_wid
                pltpu.make_async_remote_copy(
                    src_ref=p_send.at[s, j, peer],
                    dst_ref=p_got.at[s, j, d - 1],
                    send_sem=p_send_sem.at[s],
                    recv_sem=p_sem.at[s, j],
                    device_id=(hid, peer),
                    device_id_type=MESH,
                ).start()
            if with_finish:
                share(j - lag)

            @pl.when(jnp.logical_not(kept))
            def _():
                start(q + ring)

        @pl.loop(0, lag)
        def _(j):
            piece(j, False)

        @pl.loop(lag, n_up)
        def _(j):
            piece(j, True)

        def gather_hidden(first, last, sem):
            landed(
                h_got.at[s, pl.ds(first, last - first), pl.ds(0, n_wid - 1)],
                h_sems.at[s, sem],
            )
            for j in range(first, last):
                block = h_got[s, j].astype(f32)
                for half in range(2):
                    off = j * UNITS + half * LANES
                    h_all[:, off:off + LANES] = (
                        block[:, half * group:(half + 1) * group, :]
                        .reshape(n_wid * group, LANES)
                        .astype(bf16)
                    )

        def drain(first, last):
            @pl.loop(first, last)
            def _(j):
                landed(p_got.at[s, j], p_sem.at[s, j])
                finish(j)
                share(j)

        def spread(c):
            for h in range(n_hid):
                for f in range(fold):
                    branch[h, f * rows:(f + 1) * rows, :] = x_wide[
                        h * rows:(h + 1) * rows, f * LANES:(f + 1) * LANES
                    ]
            d_send[s, c] = branch[...].astype(bf16)
            d_own[c] = branch[hid]
            for d in range(1, n_hid):
                peer = (hid + d) % n_hid
                pltpu.make_async_remote_copy(
                    src_ref=d_send.at[s, c, peer],
                    dst_ref=d_got.at[s, c, d - 1],
                    send_sem=d_sems.at[s, 0],
                    recv_sem=d_sems.at[s, 1],
                    device_id=(peer, wid),
                    device_id_type=MESH,
                ).start()

        def level_slot(u, index, finish_from):
            level = levels[index]
            first, last, per = level[:3]
            depth = (last - first) * UNITS
            q = s * streamed + n_up - keep + level[4] + u
            slot = keep + q % ring
            for copy in fetch_down(u, slot, level):
                copy.wait()
            if finish_from is not None:
                j = finish_from + u
                landed(p_got.at[s, j], p_sem.at[s, j])
                finish(j)
            for part in range(per):
                c = per * u + part
                term = jnp.dot(
                    h_all[:, first * UNITS:last * UNITS],
                    slots[slot, part * depth:(part + 1) * depth, :],
                    preferred_element_type=f32,
                )
                if index == 0:
                    partial[c] = term
                elif index < len(levels) - 1:
                    partial[c] = partial[c] + term
                else:
                    x_wide[:, :cols] = partial[c] + term
                    spread(c)
            if finish_from is not None:
                share(j)
            start(q + ring)

        done = n_up - lag
        for index, level in enumerate(levels):
            need = n_up if index == len(levels) - 1 else level[1]
            if done < need:
                drain(done, need)
                done = need
            gather_hidden(level[0], level[1], index)
            more = 0 if index == len(levels) - 1 else min(level[3], n_up - done)
            if more > 0:
                pl.loop(0, more)(
                    functools.partial(level_slot, index=index, finish_from=done)
                )
                done += more
            if more < level[3]:
                pl.loop(more, level[3])(
                    functools.partial(level_slot, index=index, finish_from=None)
                )

        landed(d_got.at[s], d_sems.at[s, 1])
        total = d_own[...]
        for d in range(n_hid - 1):
            total = total + d_got[s, :, d].astype(f32)
        own[...] = (own[...] + total).astype(bf16).astype(f32)

        landed(x_got.at[s, pl.ds(0, n_hid - 1)], x_sems.at[s, 0])
        landed(p_send.at[s, :, pl.ds(0, n_wid - 1)], p_send_sem.at[s])
        landed(h_got.at[s, :, pl.ds(0, n_wid - 1)], h_sems.at[s, len(levels)])
        landed(d_send.at[s, :, pl.ds(0, n_hid - 1)], d_sems.at[s, 0])
        return carry

    lax.fori_loop(0, STEPS, step, 0)

    for c in range(n_down):
        for f in range(fold):
            off = c * cols + f * LANES
            out_wide[:, off:off + LANES] = own[c, f * rows:(f + 1) * rows, :]
    out_ref[...] = out_wide[...].astype(bf16)


def fused(n_hid, n_wid, tokens, gate_weight, up_weight, down_weight):
    rows, width = tokens.shape
    hidden = gate_weight.shape[1]
    fold = TALL // rows
    cols = fold * LANES
    n_up, n_down = hidden // UNITS, width // cols
    keep = min(KEEP, n_up - 1)
    ring = RING
    one = max(1, n_up * 5 // 13)
    two = one + max(1, (n_up - one) // 2)
    lag = min(LAG, n_up - one)
    slot_rows = max(width, UNITS * max(one, two - one, n_up - two))
    levels, before = [], 0
    for first, last in ((0, one), (one, two), (two, n_up)):
        most = min(4, slot_rows // ((last - first) * UNITS))
        per = max(p for p in range(1, most + 1) if n_down % p == 0)
        levels.append((first, last, per, n_down // per, before))
        before += n_down // per
    all_rows = n_hid * rows
    bf16, f32 = jnp.bfloat16, jnp.float32
    dma = pltpu.SemaphoreType.DMA
    weights = 3 * width * hidden
    return pl.pallas_call(
        functools.partial(kernel, n_hid, n_wid, keep, ring, lag, levels),
        out_shape=jax.ShapeDtypeStruct((rows, width), bf16),
        in_specs=[pl.BlockSpec(memory_space=pltpu.VMEM)]
        + [pl.BlockSpec(memory_space=pl.ANY)] * 3,
        out_specs=pl.BlockSpec(memory_space=pltpu.VMEM),
        scratch_shapes=[
            pltpu.VMEM((keep + ring, slot_rows, 2 * UNITS), bf16),
            pltpu.VMEM((all_rows, width), f32),
            pltpu.VMEM((all_rows, width), bf16),
            pltpu.VMEM((STEPS, n_hid, n_down, TALL, LANES), bf16),
            pltpu.VMEM((n_down, TALL, LANES), f32),
            pltpu.VMEM((all_rows, 2 * UNITS), f32),
            pltpu.VMEM((STEPS, n_up, n_wid, TALL, UNITS), bf16),
            pltpu.VMEM((STEPS, n_up, n_wid - 1, TALL, UNITS), bf16),
            pltpu.VMEM((STEPS, n_up, n_wid, TALL, LANES), bf16),
            pltpu.VMEM((all_rows, hidden), bf16),
            pltpu.VMEM((n_down, all_rows, cols), f32),
            pltpu.VMEM((n_hid, TALL, LANES), f32),
            pltpu.VMEM((STEPS, n_down, n_hid, TALL, LANES), bf16),
            pltpu.VMEM((STEPS, n_down, n_hid - 1, TALL, LANES), bf16),
            pltpu.VMEM((n_down, TALL, LANES), f32),
            pltpu.VMEM((rows, width), f32),
            dma((keep + ring, 4)),
            dma((STEPS, 2)),
            dma((STEPS,)),
            dma((STEPS, n_up)),
            dma((STEPS, len(levels) + 1)),
            dma((STEPS, 2)),
        ],
        compiler_params=pltpu.CompilerParams(
            collective_id=0, has_side_effects=True, vmem_limit_bytes=VMEM_BYTES
        ),
        cost_estimate=pl.CostEstimate(
            flops=STEPS * 2 * all_rows * weights,
            bytes_accessed=STEPS * 2 * weights,
            transcendentals=STEPS * all_rows * hidden,
        ),
    )(tokens, gate_weight, up_weight, down_weight)


VMEM_BYTES = 64 * 1024 * 1024 - 64 * 1024


def per_device(n_hid, n_wid, tokens, gate_weight, up_weight, down_weight):
    rows, width = tokens.shape
    hidden = gate_weight.shape[1]
    fits = (
        TALL % rows == 0
        and n_hid > 1
        and n_wid > 1
        and n_hid * rows == n_wid * (TALL // 2)
        and hidden % UNITS == 0
        and hidden >= 3 * UNITS
        and (TALL // rows) * LANES == 2 * UNITS
        and width % (2 * UNITS) == 0
    )
    if fits:
        return fused(n_hid, n_wid, tokens, gate_weight, up_weight, down_weight)
    return plain(tokens, gate_weight, up_weight, down_weight)


def solution(mesh):
    in_specs = (P("hid", "wid"), P("wid", "hid"), P("wid", "hid"), P("hid", "wid"))
    out_specs = P("hid", "wid")
    return jax.shard_map(
        functools.partial(per_device, mesh.shape["hid"], mesh.shape["wid"]),
        mesh=mesh,
        in_specs=in_specs,
        out_specs=out_specs,
        check_vma=False,
    )
```

```python
import functools

import jax
import jax.numpy as jnp
from jax import lax
from jax.experimental import pallas as pl
from jax.experimental.pallas import tpu as pltpu
from jax.sharding import PartitionSpec as P

STEPS = 2
MESH = pl.DeviceIdType.MESH
LANES = 128
TALL = 16
UNITS = 256
KEEP = 5
RING = 9
LAG = 5


def activate(partial_value):
    totals = lax.psum(partial_value.astype(jnp.bfloat16), "wid").astype(jnp.float32)
    return (jax.nn.silu(totals[:, 0]) * totals[:, 1]).astype(jnp.bfloat16)


def plain(tokens, gate_weight, up_weight, down_weight):
    stream = tokens
    for repeat in range(STEPS):
        shard_rows = lax.all_gather(stream, "hid", axis=0, tiled=True)
        gate_part = jnp.dot(shard_rows, gate_weight, preferred_element_type=jnp.float32)
        up_part = jnp.dot(shard_rows, up_weight, preferred_element_type=jnp.float32)
        partial_value = jnp.stack([gate_part, up_part], axis=1)
        hidden = activate(partial_value)
        branch = lax.psum_scatter(
            jnp.dot(hidden, down_weight, preferred_element_type=jnp.float32),
            "hid",
            scatter_dimension=0,
            tiled=True,
        )
        stream = (stream.astype(jnp.float32) + branch).astype(jnp.bfloat16)
    return stream


def landed(ref, sem):
    pltpu.make_async_copy(ref, ref, sem).wait()


def kernel(
    n_hid, n_wid, keep, ring, lag, levels,
    tok_ref, gate_ref, up_ref, down_ref, out_ref,
    slots, x_wide, x_all, x_got, own, product, p_send, p_got, h_got, h_all,
    partial, branch, d_send, d_got, d_own, out_wide,
    slot_sem, x_sems, p_send_sem, p_sem, h_sems, d_sems,
):
    f32, bf16 = jnp.float32, jnp.bfloat16
    hid, wid = lax.axis_index("hid"), lax.axis_index("wid")
    rows, width = tok_ref.shape
    hidden = gate_ref.shape[1]
    fold = TALL // rows
    cols = fold * LANES
    n_up, n_down = hidden // UNITS, width // cols
    group = TALL // 2
    streamed = n_up - keep + levels[-1][3] + levels[-1][4]

    def fetch_up(j, slot):
        off = pl.ds(pl.multiple_of(j * UNITS, UNITS), UNITS)
        return [
            pltpu.make_async_copy(
                ref.at[:, off],
                slots.at[slot, pl.ds(0, width), pl.ds(half * UNITS, UNITS)],
                slot_sem.at[slot, half],
            )
            for half, ref in enumerate((gate_ref, up_ref))
        ]

    def fetch_down(u, slot, level):
        first, last, per = level[:3]
        depth = (last - first) * UNITS
        return [
            pltpu.make_async_copy(
                down_ref.at[
                    pl.ds(first * UNITS, depth),
                    pl.ds(pl.multiple_of((per * u + part) * cols, cols), cols),
                ],
                slots.at[slot, pl.ds(part * depth, depth), :],
                slot_sem.at[slot, part],
            )
            for part in range(per)
        ]

    def start(q):
        slot = keep + q % ring
        k = q % streamed + keep

        @pl.when(jnp.logical_and(q < STEPS * streamed, k < n_up))
        def _():
            for copy in fetch_up(k, slot):
                copy.start()

        for level in levels:
            u = k - n_up - level[4]
            here = jnp.logical_and(u >= 0, u < level[3])

            @pl.when(jnp.logical_and(q < STEPS * streamed, here))
            def _():
                for copy in fetch_down(u, slot, level):
                    copy.start()

    @pl.loop(0, keep)
    def _(j):
        for copy in fetch_up(j, j):
            copy.start()

    @pl.loop(0, ring)
    def _(q):
        start(q)

    barrier = pltpu.get_barrier_semaphore()

    for d in range(1, n_hid):
        pl.semaphore_signal(
            barrier, inc=1, device_id=((hid + d) % n_hid, wid), device_id_type=MESH
        )
    for d in range(1, n_wid):
        pl.semaphore_signal(
            barrier, inc=1, device_id=(hid, (wid + d) % n_wid), device_id_type=MESH
        )

    for c in range(n_down):
        for f in range(fold):
            off = c * cols + f * LANES
            own[c, f * rows:(f + 1) * rows, :] = tok_ref[:, off:off + LANES].astype(f32)

    pl.semaphore_wait(barrier, n_hid + n_wid - 2)

    def step(s, carry):
        x_got[s, hid] = own[...].astype(bf16)
        for d in range(1, n_hid):
            pltpu.make_async_remote_copy(
                src_ref=x_got.at[s, hid],
                dst_ref=x_got.at[s, hid],
                send_sem=x_sems.at[s, 0],
                recv_sem=x_sems.at[s, 1],
                device_id=((hid + d) % n_hid, wid),
                device_id_type=MESH,
            ).start()
        landed(x_got.at[s, pl.ds(0, n_hid - 1)], x_sems.at[s, 1])
        for h in range(n_hid):
            for c in range(n_down):
                block = x_got[s, h, c].astype(f32)
                for f in range(fold):
                    off = c * cols + f * LANES
                    x_wide[h * rows:(h + 1) * rows, off:off + LANES] = block[
                        f * rows:(f + 1) * rows, :
                    ]
        x_all[...] = x_wide[...].astype(bf16)

        def finish(j):
            total = p_send[s, j, wid].astype(f32)
            for d in range(n_wid - 1):
                total = total + p_got[s, j, d].astype(f32)
            gate, up = total[:group, :], total[group:, :]
            value = gate / (1.0 + jnp.exp(-gate)) * up
            h_got[s, j, wid] = jnp.concatenate(
                [value[:, :LANES], value[:, LANES:]], axis=0
            ).astype(bf16)

        def share(j):
            level_of = sum(jnp.where(j >= level[0], 1, 0) for level in levels[1:])
            for d in range(1, n_wid):
                pltpu.make_async_remote_copy(
                    src_ref=h_got.at[s, j, wid],
                    dst_ref=h_got.at[s, j, wid],
                    send_sem=h_sems.at[s, len(levels)],
                    recv_sem=h_sems.at[s, level_of],
                    device_id=(hid, (wid + d) % n_wid),
                    device_id_type=MESH,
                ).start()

        def send(j):
            for d in range(1, n_wid):
                peer = (wid + d) % n_wid
                pltpu.make_async_remote_copy(
                    src_ref=p_send.at[s, j, peer],
                    dst_ref=p_got.at[s, j, d - 1],
                    send_sem=p_send_sem.at[s],
                    recv_sem=p_sem.at[s, j],
                    device_id=(hid, peer),
                    device_id_type=MESH,
                ).start()

        def piece(j, with_send, with_share, with_finish):
            q = s * streamed + j - keep
            kept = j < keep
            slot = jnp.where(kept, j, keep + (q + ring) % ring)

            @pl.when(jnp.logical_or(s == 0, jnp.logical_not(kept)))
            def _():
                for copy in fetch_up(j, slot):
                    copy.wait()

            if with_send:
                send(j - 1)
            if with_share:
                share(j - 1 - lag)
            if with_finish:
                landed(p_got.at[s, j - lag], p_sem.at[s, j - lag])
                finish(j - lag)
            product[...] = jnp.dot(
                x_all[...], slots[slot, :width, :], preferred_element_type=f32
            )
            for w in range(n_wid):
                lo = w * group
                p_send[s, j, w] = jnp.concatenate(
                    [product[lo:lo + group, :UNITS], product[lo:lo + group, UNITS:]], axis=0
                ).astype(bf16)

            @pl.when(jnp.logical_not(kept))
            def _():
                start(q + ring)

        piece(0, False, False, False)

        @pl.loop(1, lag)
        def _(j):
            piece(j, True, False, False)

        piece(lag, True, False, True)

        @pl.loop(lag + 1, n_up)
        def _(j):
            piece(j, True, True, True)

        send(n_up - 1)
        share(n_up - 1 - lag)

        def gather_hidden(first, last, sem):
            landed(
                h_got.at[s, pl.ds(first, last - first), pl.ds(0, n_wid - 1)],
                h_sems.at[s, sem],
            )
            for j in range(first, last):
                block = h_got[s, j].astype(f32)
                for half in range(2):
                    off = j * UNITS + half * LANES
                    h_all[:, off:off + LANES] = (
                        block[:, half * group:(half + 1) * group, :]
                        .reshape(n_wid * group, LANES)
                        .astype(bf16)
                    )

        def drain(first, last):
            @pl.loop(first, last)
            def _(j):
                landed(p_got.at[s, j], p_sem.at[s, j])
                finish(j)
                share(j)

        def spread(c):
            for h in range(n_hid):
                for f in range(fold):
                    branch[h, f * rows:(f + 1) * rows, :] = x_wide[
                        h * rows:(h + 1) * rows, f * LANES:(f + 1) * LANES
                    ]
            for h in range(n_hid):
                d_send[s, h, c] = branch[h].astype(bf16)
            d_own[c] = branch[hid]

        def scatter(u, per):
            part = pl.ds(per * u, per)
            for d in range(1, n_hid):
                peer = (hid + d) % n_hid
                pltpu.make_async_remote_copy(
                    src_ref=d_send.at[s, peer, part],
                    dst_ref=d_got.at[s, d - 1, part],
                    send_sem=d_sems.at[s, 0],
                    recv_sem=d_sems.at[s, 1],
                    device_id=(peer, wid),
                    device_id_type=MESH,
                ).start()

        def level_slot(u, index, finish_from):
            level = levels[index]
            first, last, per = level[:3]
            depth = (last - first) * UNITS
            q = s * streamed + n_up - keep + level[4] + u
            slot = keep + q % ring
            for copy in fetch_down(u, slot, level):
                copy.wait()
            if finish_from is not None:
                j = finish_from + u
                landed(p_got.at[s, j], p_sem.at[s, j])
                finish(j)
            for part in range(per):
                c = per * u + part
                term = jnp.dot(
                    h_all[:, first * UNITS:last * UNITS],
                    slots[slot, part * depth:(part + 1) * depth, :],
                    preferred_element_type=f32,
                )
                if index == 0:
                    partial[c] = term
                elif index < len(levels) - 1:
                    partial[c] = partial[c] + term
                else:
                    x_wide[:, :cols] = partial[c] + term
                    spread(c)
            if index == len(levels) - 1:
                scatter(u, per)
            if finish_from is not None:
                share(j)
            start(q + ring)

        done = n_up - lag
        for index, level in enumerate(levels):
            need = n_up if index == len(levels) - 1 else level[1]
            if done < need:
                drain(done, need)
                done = need
            gather_hidden(level[0], level[1], index)
            more = 0 if index == len(levels) - 1 else min(level[3], n_up - done)
            if more > 0:
                pl.loop(0, more)(
                    functools.partial(level_slot, index=index, finish_from=done)
                )
                done += more
            if more < level[3]:
                pl.loop(more, level[3])(
                    functools.partial(level_slot, index=index, finish_from=None)
                )

        landed(d_got.at[s], d_sems.at[s, 1])
        total = d_own[...]
        for d in range(n_hid - 1):
            total = total + d_got[s, d].astype(f32)
        own[...] = (own[...] + total).astype(bf16).astype(f32)

        landed(x_got.at[s, pl.ds(0, n_hid - 1)], x_sems.at[s, 0])
        landed(p_send.at[s, :, pl.ds(0, n_wid - 1)], p_send_sem.at[s])
        landed(h_got.at[s, :, pl.ds(0, n_wid - 1)], h_sems.at[s, len(levels)])
        landed(d_send.at[s, pl.ds(0, n_hid - 1)], d_sems.at[s, 0])
        return carry

    lax.fori_loop(0, STEPS, step, 0)

    for c in range(n_down):
        for f in range(fold):
            off = c * cols + f * LANES
            out_wide[:, off:off + LANES] = own[c, f * rows:(f + 1) * rows, :]
    out_ref[...] = out_wide[...].astype(bf16)


def fused(n_hid, n_wid, tokens, gate_weight, up_weight, down_weight):
    rows, width = tokens.shape
    hidden = gate_weight.shape[1]
    fold = TALL // rows
    cols = fold * LANES
    n_up, n_down = hidden // UNITS, width // cols
    keep = min(KEEP, n_up - 1)
    ring = RING
    one = max(1, n_up * 5 // 13)
    two = one + max(1, (n_up - one) * 5 // 8)
    lag = min(LAG, n_up - one)
    slot_rows = max(width, UNITS * max(one, two - one, n_up - two))
    levels, before = [], 0
    for first, last in ((0, one), (one, two), (two, n_up)):
        most = min(2 if last == n_up else 4, slot_rows // ((last - first) * UNITS))
        per = max(p for p in range(1, most + 1) if n_down % p == 0)
        levels.append((first, last, per, n_down // per, before))
        before += n_down // per
    all_rows = n_hid * rows
    bf16, f32 = jnp.bfloat16, jnp.float32
    dma = pltpu.SemaphoreType.DMA
    weights = 3 * width * hidden
    return pl.pallas_call(
        functools.partial(kernel, n_hid, n_wid, keep, ring, lag, levels),
        out_shape=jax.ShapeDtypeStruct((rows, width), bf16),
        in_specs=[pl.BlockSpec(memory_space=pltpu.VMEM)]
        + [pl.BlockSpec(memory_space=pl.ANY)] * 3,
        out_specs=pl.BlockSpec(memory_space=pltpu.VMEM),
        scratch_shapes=[
            pltpu.VMEM((keep + ring, slot_rows, 2 * UNITS), bf16),
            pltpu.VMEM((all_rows, width), f32),
            pltpu.VMEM((all_rows, width), bf16),
            pltpu.VMEM((STEPS, n_hid, n_down, TALL, LANES), bf16),
            pltpu.VMEM((n_down, TALL, LANES), f32),
            pltpu.VMEM((all_rows, 2 * UNITS), f32),
            pltpu.VMEM((STEPS, n_up, n_wid, TALL, UNITS), bf16),
            pltpu.VMEM((STEPS, n_up, n_wid - 1, TALL, UNITS), bf16),
            pltpu.VMEM((STEPS, n_up, n_wid, TALL, LANES), bf16),
            pltpu.VMEM((all_rows, hidden), bf16),
            pltpu.VMEM((n_down, all_rows, cols), f32),
            pltpu.VMEM((n_hid, TALL, LANES), f32),
            pltpu.VMEM((STEPS, n_hid, n_down, TALL, LANES), bf16),
            pltpu.VMEM((STEPS, n_hid - 1, n_down, TALL, LANES), bf16),
            pltpu.VMEM((n_down, TALL, LANES), f32),
            pltpu.VMEM((rows, width), f32),
            dma((keep + ring, 4)),
            dma((STEPS, 2)),
            dma((STEPS,)),
            dma((STEPS, n_up)),
            dma((STEPS, len(levels) + 1)),
            dma((STEPS, 2)),
        ],
        compiler_params=pltpu.CompilerParams(
            collective_id=0, has_side_effects=True, vmem_limit_bytes=VMEM_BYTES
        ),
        cost_estimate=pl.CostEstimate(
            flops=STEPS * 2 * all_rows * weights,
            bytes_accessed=STEPS * 2 * weights,
            transcendentals=STEPS * all_rows * hidden,
        ),
    )(tokens, gate_weight, up_weight, down_weight)


VMEM_BYTES = 64 * 1024 * 1024 - 64 * 1024


def per_device(n_hid, n_wid, tokens, gate_weight, up_weight, down_weight):
    rows, width = tokens.shape
    hidden = gate_weight.shape[1]
    fits = (
        TALL % rows == 0
        and n_hid > 1
        and n_wid > 1
        and n_hid * rows == n_wid * (TALL // 2)
        and hidden % UNITS == 0
        and hidden >= 3 * UNITS
        and (TALL // rows) * LANES == 2 * UNITS
        and width % (2 * UNITS) == 0
    )
    if fits:
        return fused(n_hid, n_wid, tokens, gate_weight, up_weight, down_weight)
    return plain(tokens, gate_weight, up_weight, down_weight)


def solution(mesh):
    in_specs = (P("hid", "wid"), P("wid", "hid"), P("wid", "hid"), P("hid", "wid"))
    out_specs = P("hid", "wid")
    return jax.shard_map(
        functools.partial(per_device, mesh.shape["hid"], mesh.shape["wid"]),
        mesh=mesh,
        in_specs=in_specs,
        out_specs=out_specs,
        check_vma=False,
    )
```
